32 devices in a mesh: groups: 2 (over y), tm: 8 (over z, x), cells: 2 (over core).
Axes of the slice: x: 2, y: 2, z: 4, core: 2. Of those that a mesh axis runs over, the one named last changes fastest.
Arguments:
- propagator: bfloat16 [272, 48, 4, 256], P(('groups', 'tm'), None, None, 'cells'), parts along dimension 0, as said below
- tile_blocks: int32 [272, 2], P(('groups', 'tm')), parts along dimension 0, may hold values from 0 to 15, as said below
- histories: bfloat16 [16, 12, 48], P('tm'), may hold values from -6 to 6
Outputs:
- concentration: float32 [32, 12, 4, 256], P(('groups', 'tm'), None, None, 'cells'), parts along dimension 0
The draws below stay inside these ranges and needn't reach their ends.
There are 2 independent parts, one for each index of `groups`. The reference program is written for one: setup_inputs(seed, part) draws one part's arguments, and reference() takes and returns one part's arrays. A program takes and returns all parts, laid end to end along the dimension named above; an argument that names none is the same for every part. Nothing has to cross between parts.
Inputs may be any that keep to these rules, and one draw needn't show every extreme that they name: `tile_blocks`: rows s * 17 to (s + 1) * 17 - 1 belong to two mirrored source blocks p and 15 - p, where p runs over a permutation of 0 to 7 from one such row group to the next; for each of the two source blocks every arrival block from it up to 15 appears in exactly one row, rows in any order. Tile n holds the propagator from source block tile_blocks[n, 0] to arrival block tile_blocks[n, 1].
All inputs are finite; a program needn't handle non-finite values.
Results may differ from the reference program's by a relative error of at most 0.0003.
Values may be sent and summed in bfloat16 or wider, within the bound.
A program may use at most 64 MiB of HBM per device.

```python
import jax
import jax.numpy as jnp
from jax import lax

TR = 12
BM = 4
K = 48
NB = 16
CELLS = 256
N_TM = 8


def permute_slots(slot_key):
    return jax.random.permutation(slot_key, NB + 1)


def tile_layout(key):
    pair_count = NB // 2
    slot_count = NB + 1
    order = jax.random.permutation(jax.random.fold_in(key, 11), pair_count)
    index = jnp.arange(slot_count)[None, :]
    early = order[:, None]
    late = NB - 1 - early
    first_part = index < NB - early
    sources = jnp.where(first_part, early, late)
    arrivals = jnp.where(first_part, early + index, late + index - (NB - early))
    shuffle_keys = jax.random.split(jax.random.fold_in(key, 13), pair_count)
    shuffles = jax.vmap(permute_slots)(shuffle_keys)
    sources = jnp.take_along_axis(sources, shuffles, axis=1)
    arrivals = jnp.take_along_axis(arrivals, shuffles, axis=1)
    return (sources.reshape(-1).astype(jnp.int32), arrivals.reshape(-1).astype(jnp.int32))


def draw_tile_blocks(key, part):
    sources, arrivals = tile_layout(key)
    return jnp.stack([sources, arrivals], axis=1).astype(jnp.int32)


def draw_propagator(key, part):
    sources, arrivals = tile_layout(key)
    lag = (arrivals - sources).astype(jnp.float32)
    shape = (NB // 2 * (NB + 1), K, BM, CELLS)
    noise_key = jax.random.fold_in(key, 17)
    noise = jax.random.normal(noise_key, shape, jnp.float32)
    scale = (0.15 + jnp.exp(-lag / 4.0)) / jnp.sqrt(jnp.float32(K))
    return (noise * scale[:, None, None, None]).astype(jnp.bfloat16)


def level_of(key, extent, cuts, smallest, top_value):
    def one(dim, blocks):
        steps = jax.random.uniform(jax.random.fold_in(jax.random.fold_in(key, 6), dim), (blocks,), jnp.float32, smallest / len(cuts), top_value / len(cuts))
        return jnp.repeat(jnp.exp(steps), extent[dim] // blocks).reshape((-1,) + (1,) * (len(extent) - dim - 1))

    level = one(*cuts[0])
    for cut in cuts[1:]:
        level = level * one(*cut)
    return level


def scatter_about(rng, dims, scale, bound, pieces=(), dtype=jnp.bfloat16):
    drawn = scale * jax.random.normal(rng, dims, jnp.float32)
    if pieces:
        drawn = drawn * level_of(rng, dims, pieces, -0.22, 0.18)
    return jnp.clip(drawn, -bound, bound).astype(dtype)


def setup_inputs(seed: int = 0, part: int = 0) -> dict:
    keys = jax.random.split(jax.random.key(seed), 4)
    part_splits = jax.random.split(jax.random.fold_in(keys[3], part), 4)
    return {
        "propagator": draw_propagator(jax.random.fold_in(jax.random.fold_in(keys[3], part), 71), part),
        "tile_blocks": draw_tile_blocks(jax.random.fold_in(jax.random.fold_in(keys[3], part), 71), part),
        "histories": scatter_about(keys[2], (NB, TR, K), 1.0, 6.0, ((0, 8),)),
    }


def reference(propagator, tile_blocks, histories):
    slot_count = NB + 1
    tile_sets = propagator.reshape(N_TM, slot_count, K, BM * CELLS)
    block_sets = tile_blocks.reshape(N_TM, slot_count, 2)

    def accumulate(running, element):
        tile_group, block_pairs = element
        chosen = histories[block_pairs[:, 0]].astype(jnp.float32)
        contribution = jnp.einsum('nrk,nkm->nrm', chosen, tile_group.astype(jnp.float32))
        return running.at[block_pairs[:, 1]].add(contribution), None

    running = jnp.zeros((NB, TR, BM * CELLS), jnp.float32)
    running, unused = lax.scan(accumulate, running, (tile_sets, block_sets))
    return running.reshape(NB, TR, BM, CELLS)
```

```python
import functools

import jax
import jax.numpy as jnp
from jax import lax
from jax.experimental import pallas as pl
from jax.experimental.pallas import tpu as pltpu
from jax.sharding import PartitionSpec as P

MESH = pl.DeviceIdType.MESH
HALF = 64


def steps(low, high, body):
    if high - low <= 18:
        for index in range(low, high):
            body(index)
    else:
        lax.fori_loop(low, high, lambda index, carry: (body(index), carry)[1], 0)


def iota(shape, dim):
    return lax.broadcasted_iota(jnp.int32, shape, dim)


def one_hot(condition):
    return jnp.where(condition, 1.0, 0.0).astype(jnp.bfloat16)


def dot(a, b):
    return jnp.dot(a, b, preferred_element_type=jnp.float32)


def kernel(
    n, months, prop_hbm, blocks, hist, out,
    prop, message, held, expanded, parts, outgoing, incoming, first, second,
    prop_sem, hist_send, hist_recv, part_send, part_recv,
):
    me = lax.axis_index("tm")
    slots = prop.shape[0]
    count = 2 * n
    rows = out.shape[1]
    tracers = rows // months
    width = prop.shape[1]
    months_held = hist.shape[1]

    load = pltpu.make_async_copy(prop_hbm, prop, prop_sem)
    load.start()

    barrier = pltpu.get_barrier_semaphore()

    def greet(d):
        pl.semaphore_signal(
            barrier, inc=1, device_id={"tm": lax.rem(me + d, n)}, device_id_type=MESH
        )

    steps(1, n, greet)

    pick = iota((16, 2 * tracers), 1)
    row = iota((16, 2 * tracers), 0)
    to_lane = iota((months_held, 128), 1) - iota((months_held, 128), 0)
    packed = jnp.zeros((16, 128), jnp.float32)
    for j in range(2):
        block = dot(one_hot(pick == 2 * row + j), hist[...]).astype(jnp.bfloat16)
        packed += dot(block, one_hot(to_lane == j * HALF))
    message[...] = packed.astype(jnp.bfloat16)
    held[me] = message[...]

    pl.semaphore_wait(barrier, n - 1)

    def hist_copy(d):
        return pltpu.make_async_remote_copy(
            src_ref=message,
            dst_ref=held.at[me],
            send_sem=hist_send.at[d],
            recv_sem=hist_recv.at[d],
            device_id={"tm": lax.rem(me + d, n)},
            device_id_type=MESH,
        )

    steps(1, n, lambda d: hist_copy(d).start())

    parts[slots] = jnp.zeros((rows, 128), jnp.float32)

    def find(block):
        def look(slot, found):
            newest, older = found
            hit = blocks[1, slot] == block
            return jnp.where(hit, slot, newest), jnp.where(hit, newest, older)

        found = (jnp.int32(slots), jnp.int32(slots))
        if slots <= 18:
            for slot in range(slots):
                found = look(slot, found)
        else:
            found = lax.fori_loop(0, slots, look, found)
        first[block], second[block] = found

    steps(0, count, find)

    p = blocks[0, 0]
    q = count - 1 - p
    steps(1, n, lambda d: hist_copy(d).wait_recv())
    two = jnp.concatenate([held[p // 2], held[q // 2]], axis=0)
    wide = 2 * rows
    tall_row = iota((wide, 32), 0)
    late = jnp.where(tall_row >= rows, 1, 0)
    wanted = (tall_row - late * rows) // months + 16 * late
    tall = dot(one_hot(iota((wide, 32), 1) == wanted), two)
    side = jnp.where(iota((wide, 128), 0) >= rows, q % 2, p % 2)
    tall = jnp.where(iota((wide, 128), 1) // HALF == side, tall, 0.0).astype(jnp.bfloat16)
    spread = one_hot(iota((128, width), 0) % HALF == iota((128, width), 1) // months)
    full = dot(tall, spread)
    month = iota((wide, width), 0) % months == iota((wide, width), 1) % months
    full = jnp.where(month, full, 0.0).astype(jnp.bfloat16)
    expanded[0] = full[:rows]
    expanded[1] = full[rows:]

    load.wait()

    def multiply(slot):
        which = jnp.where(blocks[0, slot] == p, 0, 1)
        parts[slot] = dot(expanded[which], prop[slot])

    steps(0, slots, multiply)

    def partial(block):
        return parts[first[block]] + parts[second[block]]

    def part_copy(d):
        return pltpu.make_async_remote_copy(
            src_ref=outgoing.at[d],
            dst_ref=incoming.at[d],
            send_sem=part_send.at[d],
            recv_sem=part_recv.at[d],
            device_id={"tm": lax.rem(me + d, n)},
            device_id_type=MESH,
        )

    def send(d):
        to = lax.rem(me + d, n)
        for j in range(2):
            outgoing[d, j] = partial(2 * to + j)
        part_copy(d).start()

    steps(1, n, send)
    for j in range(2):
        out[j] = partial(2 * me + j)

    def receive(d):
        part_copy(d).wait_recv()
        out[...] += incoming[d]

    steps(1, n, receive)

    def drain(d):
        hist_copy(d).wait_send()
        part_copy(d).wait_send()

    steps(1, n, drain)


def solution(mesh):
    n = mesh.shape["tm"]

    def shards(propagator, tile_blocks, histories):
        slots, sources, months, cells = propagator.shape
        owned, tracers, _ = histories.shape
        rows = tracers * months
        width = sources * months
        out = pl.pallas_call(
            functools.partial(kernel, n, months),
            out_shape=jax.ShapeDtypeStruct((owned, rows, cells), jnp.float32),
            in_specs=[
                pl.BlockSpec(memory_space=pltpu.HBM),
                pl.BlockSpec(memory_space=pltpu.SMEM),
                pl.BlockSpec(memory_space=pltpu.VMEM),
            ],
            out_specs=pl.BlockSpec(memory_space=pltpu.VMEM),
            scratch_shapes=[
                pltpu.VMEM((slots, width, cells), jnp.bfloat16),
                pltpu.VMEM((16, 128), jnp.bfloat16),
                pltpu.VMEM((n, 16, 128), jnp.bfloat16),
                pltpu.VMEM((2, rows, width), jnp.bfloat16),
                pltpu.VMEM((slots + 1, rows, cells), jnp.float32),
                pltpu.VMEM((n, owned, rows, cells), jnp.float32),
                pltpu.VMEM((n, owned, rows, cells), jnp.float32),
                pltpu.SMEM((2 * n,), jnp.int32),
                pltpu.SMEM((2 * n,), jnp.int32),
                pltpu.SemaphoreType.DMA,
                pltpu.SemaphoreType.DMA((n,)),
                pltpu.SemaphoreType.DMA((n,)),
                pltpu.SemaphoreType.DMA((n,)),
                pltpu.SemaphoreType.DMA((n,)),
            ],
            compiler_params=pltpu.CompilerParams(
                collective_id=0, has_side_effects=True, vmem_limit_bytes=40 * 1024 * 1024
            ),
        )(
            propagator.reshape(slots, width, cells),
            tile_blocks.T,
            histories.transpose(1, 0, 2).reshape(owned * tracers, sources),
        )
        return out.reshape(owned, tracers, months, cells)

    in_specs = (
        P(("groups", "tm"), None, None, "cells"),
        P(("groups", "tm"), None),
        P("tm", None, None),
    )
    out_specs = P(("groups", "tm"), None, None, "cells")
    return jax.shard_map(shards, mesh=mesh, in_specs=in_specs, out_specs=out_specs, check_vma=False)
```

```python
import functools

import jax
import jax.numpy as jnp
from jax import lax
from jax.experimental import pallas as pl
from jax.experimental.pallas import tpu as pltpu
from jax.sharding import PartitionSpec as P

MESH = pl.DeviceIdType.MESH
HALF = 64


def steps(low, high, body):
    if high - low <= 18:
        for index in range(low, high):
            body(index)
    else:
        lax.fori_loop(low, high, lambda index, carry: (body(index), carry)[1], 0)


def iota(shape, dim):
    return lax.broadcasted_iota(jnp.int32, shape, dim)


def one_hot(condition):
    return jnp.where(condition, 1.0, 0.0).astype(jnp.bfloat16)


def dot(a, b):
    return jnp.dot(a, b, preferred_element_type=jnp.float32)


def kernel(
    n, months, prop_hbm, blocks_hbm, hist_hbm, out,
    prop, blocks, hist, message, held, expanded, parts, outgoing, incoming, first, second,
    prop_sem, blocks_sem, hist_sem, hist_send, hist_recv, part_send, part_recv,
):
    me = lax.axis_index("tm")
    slots = prop.shape[0]
    count = 2 * n
    rows = out.shape[1]
    tracers = rows // months
    width = prop.shape[1]
    months_held = hist.shape[1]

    load_hist = pltpu.make_async_copy(hist_hbm, hist, hist_sem)
    load_hist.start()
    load_blocks = pltpu.make_async_copy(blocks_hbm, blocks, blocks_sem)
    load_blocks.start()
    load = pltpu.make_async_copy(prop_hbm, prop, prop_sem)
    load.start()

    barrier = pltpu.get_barrier_semaphore()

    def greet(d):
        pl.semaphore_signal(
            barrier, inc=1, device_id={"tm": lax.rem(me + d, n)}, device_id_type=MESH
        )

    steps(1, n, greet)

    pick = iota((16, 2 * tracers), 1)
    row = iota((16, 2 * tracers), 0)
    to_lane = iota((months_held, 128), 1) - iota((months_held, 128), 0)
    load_hist.wait()
    packed = jnp.zeros((16, 128), jnp.float32)
    for j in range(2):
        block = dot(one_hot(pick == 2 * row + j), hist[...]).astype(jnp.bfloat16)
        packed += dot(block, one_hot(to_lane == j * HALF))
    message[...] = packed.astype(jnp.bfloat16)
    held[me] = message[...]

    pl.semaphore_wait(barrier, n - 1)

    def hist_copy(d):
        return pltpu.make_async_remote_copy(
            src_ref=message,
            dst_ref=held.at[me],
            send_sem=hist_send.at[d],
            recv_sem=hist_recv.at[d],
            device_id={"tm": lax.rem(me + d, n)},
            device_id_type=MESH,
        )

    steps(1, n, lambda d: hist_copy(d).start())

    load_blocks.wait()

    parts[slots] = jnp.zeros((rows, 128), jnp.float32)

    def find(block):
        def look(slot, found):
            newest, older = found
            hit = blocks[1, slot] == block
            return jnp.where(hit, slot, newest), jnp.where(hit, newest, older)

        found = (jnp.int32(slots), jnp.int32(slots))
        if slots <= 18:
            for slot in range(slots):
                found = look(slot, found)
        else:
            found = lax.fori_loop(0, slots, look, found)
        first[block], second[block] = found

    steps(0, count, find)

    p = blocks[0, 0]
    q = count - 1 - p
    steps(1, n, lambda d: hist_copy(d).wait_recv())
    two = jnp.concatenate([held[p // 2], held[q // 2]], axis=0)
    wide = 2 * rows
    tall_row = iota((wide, 32), 0)
    late = jnp.where(tall_row >= rows, 1, 0)
    wanted = (tall_row - late * rows) // months + 16 * late
    tall = dot(one_hot(iota((wide, 32), 1) == wanted), two)
    side = jnp.where(iota((wide, 128), 0) >= rows, q % 2, p % 2)
    tall = jnp.where(iota((wide, 128), 1) // HALF == side, tall, 0.0).astype(jnp.bfloat16)
    spread = one_hot(iota((128, width), 0) % HALF == iota((128, width), 1) // months)
    full = dot(tall, spread)
    month = iota((wide, width), 0) % months == iota((wide, width), 1) % months
    full = jnp.where(month, full, 0.0).astype(jnp.bfloat16)
    expanded[0] = full[:rows]
    expanded[1] = full[rows:]

    load.wait()

    def multiply(slot):
        which = jnp.where(blocks[0, slot] == p, 0, 1)
        parts[slot] = dot(expanded[which], prop[slot])

    steps(0, slots, multiply)

    def partial(block):
        return parts[first[block]] + parts[second[block]]

    def part_copy(d):
        return pltpu.make_async_remote_copy(
            src_ref=outgoing.at[d],
            dst_ref=incoming.at[d],
            send_sem=part_send.at[d],
            recv_sem=part_recv.at[d],
            device_id={"tm": lax.rem(me + d, n)},
            device_id_type=MESH,
        )

    def send(d):
        to = lax.rem(me + d, n)
        for j in range(2):
            outgoing[d, j] = partial(2 * to + j)
        part_copy(d).start()

    steps(1, n, send)
    for j in range(2):
        out[j] = partial(2 * me + j)

    def receive(d):
        part_copy(d).wait_recv()
        out[...] += incoming[d]

    steps(1, n, receive)

    def drain(d):
        hist_copy(d).wait_send()
        part_copy(d).wait_send()

    steps(1, n, drain)


def solution(mesh):
    n = mesh.shape["tm"]

    def shards(propagator, tile_blocks, histories):
        slots, sources, months, cells = propagator.shape
        owned, tracers, _ = histories.shape
        rows = tracers * months
        width = sources * months
        out = pl.pallas_call(
            functools.partial(kernel, n, months),
            out_shape=jax.ShapeDtypeStruct((owned, rows, cells), jnp.float32),
            in_specs=[
                pl.BlockSpec(memory_space=pltpu.HBM),
                pl.BlockSpec(memory_space=pltpu.HBM),
                pl.BlockSpec(memory_space=pltpu.HBM),
            ],
            out_specs=pl.BlockSpec(memory_space=pltpu.VMEM),
            scratch_shapes=[
                pltpu.VMEM((slots, width, cells), jnp.bfloat16),
                pltpu.SMEM((2, slots), jnp.int32),
                pltpu.VMEM((owned * tracers, sources), jnp.bfloat16),
                pltpu.VMEM((16, 128), jnp.bfloat16),
                pltpu.VMEM((n, 16, 128), jnp.bfloat16),
                pltpu.VMEM((2, rows, width), jnp.bfloat16),
                pltpu.VMEM((slots + 1, rows, cells), jnp.float32),
                pltpu.VMEM((n, owned, rows, cells), jnp.float32),
                pltpu.VMEM((n, owned, rows, cells), jnp.float32),
                pltpu.SMEM((2 * n,), jnp.int32),
                pltpu.SMEM((2 * n,), jnp.int32),
                pltpu.SemaphoreType.DMA,
                pltpu.SemaphoreType.DMA,
                pltpu.SemaphoreType.DMA,
                pltpu.SemaphoreType.DMA((n,)),
                pltpu.SemaphoreType.DMA((n,)),
                pltpu.SemaphoreType.DMA((n,)),
                pltpu.SemaphoreType.DMA((n,)),
            ],
            compiler_params=pltpu.CompilerParams(
                collective_id=0, has_side_effects=True, vmem_limit_bytes=63 * 1024 * 1024
            ),
        )(
            propagator.reshape(slots, width, cells),
            tile_blocks.T,
            histories.transpose(1, 0, 2).reshape(owned * tracers, sources),
        )
        return out.reshape(owned, tracers, months, cells)

    in_specs = (
        P(("groups", "tm"), None, None, "cells"),
        P(("groups", "tm"), None),
        P("tm", None, None),
    )
    out_specs = P(("groups", "tm"), None, None, "cells")
    return jax.shard_map(shards, mesh=mesh, in_specs=in_specs, out_specs=out_specs, check_vma=False)
```

```python
import functools

import jax
import jax.numpy as jnp
from jax import lax
from jax.experimental import pallas as pl
from jax.experimental.pallas import tpu as pltpu
from jax.sharding import PartitionSpec as P

MESH = pl.DeviceIdType.MESH
HALF = 64


def steps(low, high, body):
    if high - low <= 18:
        for index in range(low, high):
            body(index)
    else:
        lax.fori_loop(low, high, lambda index, carry: (body(index), carry)[1], 0)


def iota(shape, dim):
    return lax.broadcasted_iota(jnp.int32, shape, dim)


def one_hot(condition):
    return jnp.where(condition, 1.0, 0.0).astype(jnp.bfloat16)


def dot(a, b):
    return jnp.dot(a, b, preferred_element_type=jnp.float32)


def encode(values):
    groups = values.reshape(-1, 8, 128)
    largest = jnp.max(jnp.abs(groups), axis=0)
    exponent = jnp.floor(jnp.log2(jnp.maximum(largest, 1e-37)))
    half = jnp.exp2(-0.5 * exponent)
    scaled = groups * half * half * 16384.0
    code = jnp.clip(jnp.floor(scaled + 0.5), -32767.0, 32767.0).astype(jnp.int32)
    tail = jnp.concatenate([exponent, exponent], axis=0).astype(jnp.int32)
    return code.reshape(-1, 128).astype(jnp.int16), tail.astype(jnp.int16)


def decode(code, tail):
    half = jnp.exp2(0.5 * tail.astype(jnp.int32).astype(jnp.float32)[:8])
    groups = code.astype(jnp.int32).astype(jnp.float32).reshape(-1, 8, 128)
    return (groups * (1.0 / 16384.0) * half * half).reshape(2, -1, 128)


def kernel(
    n, months, prop_hbm, blocks_hbm, hist_hbm, out,
    prop, blocks, hist, message, held, expanded, parts, outgoing, incoming, first, second,
    prop_sem, blocks_sem, hist_sem, hist_send, hist_recv, part_send, part_recv,
):
    me = lax.axis_index("tm")
    slots = prop.shape[0]
    count = 2 * n
    rows = out.shape[1]
    tracers = rows // months
    width = prop.shape[1]
    months_held = hist.shape[1]

    load_hist = pltpu.make_async_copy(hist_hbm, hist, hist_sem)
    load_hist.start()
    load_blocks = pltpu.make_async_copy(blocks_hbm, blocks, blocks_sem)
    load_blocks.start()
    load = pltpu.make_async_copy(prop_hbm, prop, prop_sem)
    load.start()

    barrier = pltpu.get_barrier_semaphore()

    def greet(d):
        pl.semaphore_signal(
            barrier, inc=1, device_id={"tm": lax.rem(me + d, n)}, device_id_type=MESH
        )

    steps(1, n, greet)

    pick = iota((16, 2 * tracers), 1)
    row = iota((16, 2 * tracers), 0)
    to_lane = iota((months_held, 128), 1) - iota((months_held, 128), 0)
    load_hist.wait()
    packed = jnp.zeros((16, 128), jnp.float32)
    for j in range(2):
        block = dot(one_hot(pick == 2 * row + j), hist[...]).astype(jnp.bfloat16)
        packed += dot(block, one_hot(to_lane == j * HALF))
    message[...] = packed.astype(jnp.bfloat16)
    held[me] = message[...]

    pl.semaphore_wait(barrier, n - 1)

    def hist_copy(d):
        return pltpu.make_async_remote_copy(
            src_ref=message,
            dst_ref=held.at[me],
            send_sem=hist_send.at[d],
            recv_sem=hist_recv.at[d],
            device_id={"tm": lax.rem(me + d, n)},
            device_id_type=MESH,
        )

    steps(1, n, lambda d: hist_copy(d).start())

    load_blocks.wait()

    parts[slots] = jnp.zeros((rows, 128), jnp.float32)

    def find(block):
        def look(slot, found):
            newest, older = found
            hit = blocks[1, slot] == block
            return jnp.where(hit, slot, newest), jnp.where(hit, newest, older)

        found = (jnp.int32(slots), jnp.int32(slots))
        if slots <= 18:
            for slot in range(slots):
                found = look(slot, found)
        else:
            found = lax.fori_loop(0, slots, look, found)
        first[block], second[block] = found

    steps(0, count, find)

    p = blocks[0, 0]
    q = count - 1 - p
    steps(1, n, lambda d: hist_copy(d).wait_recv())
    two = jnp.concatenate([held[p // 2], held[q // 2]], axis=0)
    wide = 2 * rows
    tall_row = iota((wide, 32), 0)
    late = jnp.where(tall_row >= rows, 1, 0)
    wanted = (tall_row - late * rows) // months + 16 * late
    tall = dot(one_hot(iota((wide, 32), 1) == wanted), two)
    side = jnp.where(iota((wide, 128), 0) >= rows, q % 2, p % 2)
    tall = jnp.where(iota((wide, 128), 1) // HALF == side, tall, 0.0).astype(jnp.bfloat16)
    spread = one_hot(iota((128, width), 0) % HALF == iota((128, width), 1) // months)
    full = dot(tall, spread)
    month = iota((wide, width), 0) % months == iota((wide, width), 1) % months
    full = jnp.where(month, full, 0.0).astype(jnp.bfloat16)
    expanded[0] = full[:rows]
    expanded[1] = full[rows:]

    load.wait()

    def multiply(slot):
        which = jnp.where(blocks[0, slot] == p, 0, 1)
        parts[slot] = dot(expanded[which], prop[slot])

    steps(0, slots, multiply)

    def partial(block):
        return parts[first[block]] + parts[second[block]]

    def part_copy(d):
        return pltpu.make_async_remote_copy(
            src_ref=outgoing.at[d],
            dst_ref=incoming.at[d],
            send_sem=part_send.at[d],
            recv_sem=part_recv.at[d],
            device_id={"tm": lax.rem(me + d, n)},
            device_id_type=MESH,
        )

    def send(d):
        to = lax.rem(me + d, n)
        both = jnp.concatenate([partial(2 * to), partial(2 * to + 1)], axis=0)
        code, tail = encode(both)
        outgoing[d, : 2 * rows] = code
        outgoing[d, 2 * rows :] = tail
        part_copy(d).start()

    steps(1, n, send)
    for j in range(2):
        out[j] = partial(2 * me + j)

    def receive(d):
        part_copy(d).wait_recv()
        out[...] += decode(incoming[d, : 2 * rows], incoming[d, 2 * rows :])

    steps(1, n, receive)

    def drain(d):
        hist_copy(d).wait_send()
        part_copy(d).wait_send()

    steps(1, n, drain)


def solution(mesh):
    n = mesh.shape["tm"]

    def shards(propagator, tile_blocks, histories):
        slots, sources, months, cells = propagator.shape
        owned, tracers, _ = histories.shape
        rows = tracers * months
        width = sources * months
        out = pl.pallas_call(
            functools.partial(kernel, n, months),
            out_shape=jax.ShapeDtypeStruct((owned, rows, cells), jnp.float32),
            in_specs=[
                pl.BlockSpec(memory_space=pltpu.HBM),
                pl.BlockSpec(memory_space=pltpu.HBM),
                pl.BlockSpec(memory_space=pltpu.HBM),
            ],
            out_specs=pl.BlockSpec(memory_space=pltpu.VMEM),
            scratch_shapes=[
                pltpu.VMEM((slots, width, cells), jnp.bfloat16),
                pltpu.SMEM((2, slots), jnp.int32),
                pltpu.VMEM((owned * tracers, sources), jnp.bfloat16),
                pltpu.VMEM((16, 128), jnp.bfloat16),
                pltpu.VMEM((n, 16, 128), jnp.bfloat16),
                pltpu.VMEM((2, rows, width), jnp.bfloat16),
                pltpu.VMEM((slots + 1, rows, cells), jnp.float32),
                pltpu.VMEM((n, owned * rows + 16, cells), jnp.int16),
                pltpu.VMEM((n, owned * rows + 16, cells), jnp.int16),
                pltpu.SMEM((2 * n,), jnp.int32),
                pltpu.SMEM((2 * n,), jnp.int32),
                pltpu.SemaphoreType.DMA,
                pltpu.SemaphoreType.DMA,
                pltpu.SemaphoreType.DMA,
                pltpu.SemaphoreType.DMA((n,)),
                pltpu.SemaphoreType.DMA((n,)),
                pltpu.SemaphoreType.DMA((n,)),
                pltpu.SemaphoreType.DMA((n,)),
            ],
            compiler_params=pltpu.CompilerParams(
                collective_id=0, has_side_effects=True, vmem_limit_bytes=63 * 1024 * 1024
            ),
        )(
            propagator.reshape(slots, width, cells),
            tile_blocks.T,
            histories.transpose(1, 0, 2).reshape(owned * tracers, sources),
        )
        return out.reshape(owned, tracers, months, cells)

    in_specs = (
        P(("groups", "tm"), None, None, "cells"),
        P(("groups", "tm"), None),
        P("tm", None, None),
    )
    out_specs = P(("groups", "tm"), None, None, "cells")
    return jax.shard_map(shards, mesh=mesh, in_specs=in_specs, out_specs=out_specs, check_vma=False)
```

```python
import functools

import jax
import jax.numpy as jnp
from jax import lax
from jax.experimental import pallas as pl
from jax.experimental.pallas import tpu as pltpu
from jax.sharding import PartitionSpec as P

MESH = pl.DeviceIdType.MESH
HALF = 64


def steps(low, high, body):
    if high - low <= 18:
        for index in range(low, high):
            body(index)
    else:
        lax.fori_loop(low, high, lambda index, carry: (body(index), carry)[1], 0)


def iota(shape, dim):
    return lax.broadcasted_iota(jnp.int32, shape, dim)


def one_hot(condition):
    return jnp.where(condition, 1.0, 0.0).astype(jnp.bfloat16)


def dot(a, b):
    return jnp.dot(a, b, preferred_element_type=jnp.float32)


def encode(values):
    groups = values.reshape(-1, 8, 128)
    largest = jnp.max(jnp.abs(groups), axis=0)
    exponent = jnp.floor(jnp.log2(jnp.maximum(largest, 1e-37)))
    half = jnp.exp2(-0.5 * exponent)
    scaled = groups * half * half * 16384.0
    code = jnp.clip(jnp.floor(scaled + 0.5), -32767.0, 32767.0).astype(jnp.int32)
    tail = jnp.concatenate([exponent, exponent], axis=0).astype(jnp.int32)
    return code.reshape(-1, 128).astype(jnp.int16), tail.astype(jnp.int16)


def decode(code, tail):
    half = jnp.exp2(0.5 * tail.astype(jnp.int32).astype(jnp.float32)[:8])
    groups = code.astype(jnp.int32).astype(jnp.float32).reshape(-1, 8, 128)
    return (groups * (1.0 / 16384.0) * half * half).reshape(2, -1, 128)


def kernel(
    n, months, prop_hbm, blocks_hbm, hist_hbm, out,
    prop, blocks, hist, message, held, expanded, parts, outgoing, incoming, first, second,
    prop_sem, blocks_sem, hist_sem, hist_send, hist_recv, part_send, part_recv,
):
    me = lax.axis_index("tm")
    slots = prop.shape[0]
    count = 2 * n
    rows = out.shape[1]
    tracers = rows // months
    width = prop.shape[1]
    months_held = hist.shape[1]

    load_hist = pltpu.make_async_copy(hist_hbm, hist, hist_sem)
    load_hist.start()
    load_blocks = pltpu.make_async_copy(blocks_hbm, blocks, blocks_sem)
    load_blocks.start()
    load = pltpu.make_async_copy(prop_hbm, prop, prop_sem)
    load.start()

    barrier = pltpu.get_barrier_semaphore()

    def greet(d):
        pl.semaphore_signal(
            barrier, inc=1, device_id={"tm": lax.rem(me + d, n)}, device_id_type=MESH
        )

    steps(1, n, greet)

    pick = iota((16, 2 * tracers), 1)
    row = iota((16, 2 * tracers), 0)
    to_lane = iota((months_held, 128), 1) - iota((months_held, 128), 0)
    load_hist.wait()
    packed = jnp.zeros((16, 128), jnp.float32)
    for j in range(2):
        block = dot(one_hot(pick == 2 * row + j), hist[...]).astype(jnp.bfloat16)
        packed += dot(block, one_hot(to_lane == j * HALF))
    message[...] = packed.astype(jnp.bfloat16)
    held[me] = message[...]

    pl.semaphore_wait(barrier, n - 1)

    def hist_copy(d):
        return pltpu.make_async_remote_copy(
            src_ref=message,
            dst_ref=held.at[me],
            send_sem=hist_send.at[d],
            recv_sem=hist_recv.at[d],
            device_id={"tm": lax.rem(me + d, n)},
            device_id_type=MESH,
        )

    steps(1, n, lambda d: hist_copy(d).start())

    load_blocks.wait()

    parts[slots] = jnp.zeros((rows, 128), jnp.float32)

    def find(block):
        def look(slot, found):
            newest, older = found
            hit = blocks[1, slot] == block
            return jnp.where(hit, slot, newest), jnp.where(hit, newest, older)

        found = (jnp.int32(slots), jnp.int32(slots))
        if slots <= 18:
            for slot in range(slots):
                found = look(slot, found)
        else:
            found = lax.fori_loop(0, slots, look, found)
        first[block], second[block] = found

    steps(0, count, find)

    p = blocks[0, 0]
    q = count - 1 - p
    steps(1, n, lambda d: hist_copy(d).wait_recv())
    two = jnp.concatenate([held[p // 2], held[q // 2]], axis=0)
    wide = 2 * rows
    tall_row = iota((wide, 32), 0)
    late = jnp.where(tall_row >= rows, 1, 0)
    wanted = (tall_row - late * rows) // months + 16 * late
    tall = dot(one_hot(iota((wide, 32), 1) == wanted), two)
    side = jnp.where(iota((wide, 128), 0) >= rows, q % 2, p % 2)
    tall = jnp.where(iota((wide, 128), 1) // HALF == side, tall, 0.0).astype(jnp.bfloat16)
    spread = one_hot(iota((128, width), 0) % HALF == iota((128, width), 1) // months)
    full = dot(tall, spread)
    month = iota((wide, width), 0) % months == iota((wide, width), 1) % months
    full = jnp.where(month, full, 0.0).astype(jnp.bfloat16)
    expanded[0] = full[:rows]
    expanded[1] = full[rows:]

    load.wait()

    def multiply(slot):
        which = jnp.where(blocks[0, slot] == p, 0, 1)
        parts[slot] = dot(expanded[which], prop[slot])

    steps(0, slots, multiply)

    def partial(block):
        return parts[first[block]] + parts[second[block]]

    def part_copy(d):
        return pltpu.make_async_remote_copy(
            src_ref=outgoing.at[d],
            dst_ref=incoming.at[d],
            send_sem=part_send.at[d],
            recv_sem=part_recv.at[d],
            device_id={"tm": lax.rem(me + d, n)},
            device_id_type=MESH,
        )

    def send(d):
        to = lax.rem(me + d, n)
        both = jnp.concatenate([partial(2 * to), partial(2 * to + 1)], axis=0)
        code, tail = encode(both)
        outgoing[d, : 2 * rows] = code
        outgoing[d, 2 * rows :] = tail
        part_copy(d).start()

    steps(1, n, send)
    for j in range(2):
        out[j] = partial(2 * me + j)

    def receive(d):
        part_copy(d).wait_recv()
        out[...] += decode(incoming[d, : 2 * rows], incoming[d, 2 * rows :])

    steps(1, n, receive)

    def drain(d):
        hist_copy(d).wait_send()
        part_copy(d).wait_send()

    steps(1, n, drain)


def solution(mesh):
    n = mesh.shape["tm"]

    def shards(propagator, tile_blocks, histories):
        slots, sources, months, cells = propagator.shape
        owned, tracers, _ = histories.shape
        rows = tracers * months
        width = sources * months
        out = pl.pallas_call(
            functools.partial(kernel, n, months),
            out_shape=pltpu.VMEM((owned, rows, cells), jnp.float32),
            in_specs=[
                pl.BlockSpec(memory_space=pltpu.HBM),
                pl.BlockSpec(memory_space=pltpu.HBM),
                pl.BlockSpec(memory_space=pltpu.HBM),
            ],
            out_specs=pl.BlockSpec(memory_space=pltpu.VMEM),
            scratch_shapes=[
                pltpu.VMEM((slots, width, cells), jnp.bfloat16),
                pltpu.SMEM((2, slots), jnp.int32),
                pltpu.VMEM((owned * tracers, sources), jnp.bfloat16),
                pltpu.VMEM((16, 128), jnp.bfloat16),
                pltpu.VMEM((n, 16, 128), jnp.bfloat16),
                pltpu.VMEM((2, rows, width), jnp.bfloat16),
                pltpu.VMEM((slots + 1, rows, cells), jnp.float32),
                pltpu.VMEM((n, owned * rows + 16, cells), jnp.int16),
                pltpu.VMEM((n, owned * rows + 16, cells), jnp.int16),
                pltpu.SMEM((2 * n,), jnp.int32),
                pltpu.SMEM((2 * n,), jnp.int32),
                pltpu.SemaphoreType.DMA,
                pltpu.SemaphoreType.DMA,
                pltpu.SemaphoreType.DMA,
                pltpu.SemaphoreType.DMA((n,)),
                pltpu.SemaphoreType.DMA((n,)),
                pltpu.SemaphoreType.DMA((n,)),
                pltpu.SemaphoreType.DMA((n,)),
            ],
            compiler_params=pltpu.CompilerParams(
                collective_id=0, has_side_effects=True, vmem_limit_bytes=63 * 1024 * 1024
            ),
        )(
            propagator.reshape(slots, width, cells),
            tile_blocks.T,
            histories.transpose(1, 0, 2).reshape(owned * tracers, sources),
        )
        return out.reshape(owned, tracers, months, cells)

    in_specs = (
        P(("groups", "tm"), None, None, "cells"),
        P(("groups", "tm"), None),
        P("tm", None, None),
    )
    out_specs = P(("groups", "tm"), None, None, "cells")
    return jax.shard_map(shards, mesh=mesh, in_specs=in_specs, out_specs=out_specs, check_vma=False)
```

```python
import functools

import jax
import jax.numpy as jnp
from jax import lax
from jax.experimental import pallas as pl
from jax.experimental.pallas import tpu as pltpu
from jax.sharding import PartitionSpec as P

MESH = pl.DeviceIdType.MESH
HALF = 64


def steps(low, high, body):
    if high - low <= 18:
        for index in reversed(range(low, high)):
            body(index)
    else:
        lax.fori_loop(low, high, lambda index, carry: (body(index), carry)[1], 0)


def iota(shape, dim):
    return lax.broadcasted_iota(jnp.int32, shape, dim)


def one_hot(condition):
    return jnp.where(condition, 1.0, 0.0).astype(jnp.bfloat16)


def dot(a, b):
    return jnp.dot(a, b, preferred_element_type=jnp.float32)


def encode(values):
    groups = values.reshape(-1, 8, 128)
    largest = jnp.max(jnp.abs(groups), axis=0)
    exponent = jnp.floor(jnp.log2(jnp.maximum(largest, 1e-37)))
    half = jnp.exp2(-0.5 * exponent)
    bits = exponent.astype(jnp.int32) + 128
    coded = []
    for i in range(groups.shape[0]):
        scaled = groups[i] * half * half * 8192.0
        code = jnp.clip(jnp.floor(scaled + 0.5), -16383.0, 16383.0).astype(jnp.int32) * 2
        if i < 8:
            code = code + ((bits >> i) & 1)
        coded.append(code)
    return jnp.concatenate(coded, axis=0).astype(jnp.int16)


def decode(code):
    groups = code.astype(jnp.int32).reshape(-1, 8, 128)
    low = groups & 1
    bits = low[0]
    for i in range(1, 8):
        bits = bits + (low[i] << i)
    half = jnp.exp2(0.5 * (bits - 128).astype(jnp.float32))
    values = (groups - low).astype(jnp.float32) * (1.0 / 16384.0) * half * half
    return values.reshape(2, -1, 128)


def partner(me, d, n):
    if n & (n - 1):
        return lax.rem(me + d, n)
    other, bit = 0, 1
    while bit < n:
        other = other + bit * ((me // bit + d // bit) % 2)
        bit *= 2
    return other


def kernel(
    n, months, prop_hbm, blocks_hbm, hist_hbm, out,
    prop, blocks, hist, message, held, expanded, parts, outgoing, incoming, first, second,
    prop_sem, blocks_sem, hist_sem, hist_send, hist_recv, part_send, part_recv,
):
    me = lax.axis_index("tm")
    slots = prop.shape[0]
    count = 2 * n
    rows = out.shape[1]
    tracers = rows // months
    width = prop.shape[1]
    months_held = hist.shape[1]

    load_hist = pltpu.make_async_copy(hist_hbm, hist, hist_sem)
    load_hist.start()
    load_blocks = pltpu.make_async_copy(blocks_hbm, blocks, blocks_sem)
    load_blocks.start()
    load = pltpu.make_async_copy(prop_hbm, prop, prop_sem)
    load.start()

    barrier = pltpu.get_barrier_semaphore()

    def greet(d):
        pl.semaphore_signal(
            barrier, inc=1, device_id={"tm": partner(me, d, n)}, device_id_type=MESH
        )

    steps(1, n, greet)

    pick = iota((16, 2 * tracers), 1)
    row = iota((16, 2 * tracers), 0)
    to_lane = iota((months_held, 128), 1) - iota((months_held, 128), 0)
    load_hist.wait()
    packed = jnp.zeros((16, 128), jnp.float32)
    for j in range(2):
        block = dot(one_hot(pick == 2 * row + j), hist[...]).astype(jnp.bfloat16)
        packed += dot(block, one_hot(to_lane == j * HALF))
    message[...] = packed.astype(jnp.bfloat16)
    held[me] = message[...]

    pl.semaphore_wait(barrier, n - 1)

    def hist_copy(d):
        return pltpu.make_async_remote_copy(
            src_ref=message,
            dst_ref=held.at[me],
            send_sem=hist_send.at[d],
            recv_sem=hist_recv.at[d],
            device_id={"tm": partner(me, d, n)},
            device_id_type=MESH,
        )

    steps(1, n, lambda d: hist_copy(d).start())

    load_blocks.wait()

    parts[slots] = jnp.zeros((rows, 128), jnp.float32)

    def find(block):
        def look(slot, found):
            newest, older = found
            hit = blocks[1, slot] == block
            return jnp.where(hit, slot, newest), jnp.where(hit, newest, older)

        found = (jnp.int32(slots), jnp.int32(slots))
        if slots <= 18:
            for slot in range(slots):
                found = look(slot, found)
        else:
            found = lax.fori_loop(0, slots, look, found)
        first[block], second[block] = found

    steps(0, count, find)

    p = blocks[0, 0]
    q = count - 1 - p
    steps(1, n, lambda d: hist_copy(d).wait_recv())
    two = jnp.concatenate([held[p // 2], held[q // 2]], axis=0)
    wide = 2 * rows
    tall_row = iota((wide, 32), 0)
    late = jnp.where(tall_row >= rows, 1, 0)
    wanted = (tall_row - late * rows) // months + 16 * late
    tall = dot(one_hot(iota((wide, 32), 1) == wanted), two)
    side = jnp.where(iota((wide, 128), 0) >= rows, q % 2, p % 2)
    tall = jnp.where(iota((wide, 128), 1) // HALF == side, tall, 0.0).astype(jnp.bfloat16)
    spread = one_hot(iota((128, width), 0) % HALF == iota((128, width), 1) // months)
    full = dot(tall, spread)
    month = iota((wide, width), 0) % months == iota((wide, width), 1) % months
    full = jnp.where(month, full, 0.0).astype(jnp.bfloat16)
    expanded[0] = full[:rows]
    expanded[1] = full[rows:]

    load.wait()

    def multiply(slot):
        which = jnp.where(blocks[0, slot] == p, 0, 1)
        parts[slot] = dot(expanded[which], prop[slot])

    steps(0, slots, multiply)

    def partial(block):
        return parts[first[block]] + parts[second[block]]

    def part_copy(d):
        return pltpu.make_async_remote_copy(
            src_ref=outgoing.at[d],
            dst_ref=incoming.at[d],
            send_sem=part_send.at[d],
            recv_sem=part_recv.at[d],
            device_id={"tm": partner(me, d, n)},
            device_id_type=MESH,
        )

    def send(d):
        to = partner(me, d, n)
        both = jnp.concatenate([partial(2 * to), partial(2 * to + 1)], axis=0)
        outgoing[d] = encode(both)
        part_copy(d).start()

    steps(1, n, send)
    for j in range(2):
        out[j] = partial(2 * me + j)

    def receive(d):
        part_copy(d).wait_recv()
        out[...] += decode(incoming[d])

    steps(1, n, receive)

    def drain(d):
        hist_copy(d).wait_send()
        part_copy(d).wait_send()

    steps(1, n, drain)


def solution(mesh):
    n = mesh.shape["tm"]

    def shards(propagator, tile_blocks, histories):
        slots, sources, months, cells = propagator.shape
        owned, tracers, _ = histories.shape
        rows = tracers * months
        width = sources * months
        out = pl.pallas_call(
            functools.partial(kernel, n, months),
            out_shape=pltpu.VMEM((owned, rows, cells), jnp.float32),
            in_specs=[
                pl.BlockSpec(memory_space=pltpu.HBM),
                pl.BlockSpec(memory_space=pltpu.HBM),
                pl.BlockSpec(memory_space=pltpu.HBM),
            ],
            out_specs=pl.BlockSpec(memory_space=pltpu.VMEM),
            scratch_shapes=[
                pltpu.VMEM((slots, width, cells), jnp.bfloat16),
                pltpu.SMEM((2, slots), jnp.int32),
                pltpu.VMEM((owned * tracers, sources), jnp.bfloat16),
                pltpu.VMEM((16, 128), jnp.bfloat16),
                pltpu.VMEM((n, 16, 128), jnp.bfloat16),
                pltpu.VMEM((2, rows, width), jnp.bfloat16),
                pltpu.VMEM((slots + 1, rows, cells), jnp.float32),
                pltpu.VMEM((n, owned * rows, cells), jnp.int16),
                pltpu.VMEM((n, owned * rows, cells), jnp.int16),
                pltpu.SMEM((2 * n,), jnp.int32),
                pltpu.SMEM((2 * n,), jnp.int32),
                pltpu.SemaphoreType.DMA,
                pltpu.SemaphoreType.DMA,
                pltpu.SemaphoreType.DMA,
                pltpu.SemaphoreType.DMA((n,)),
                pltpu.SemaphoreType.DMA((n,)),
                pltpu.SemaphoreType.DMA((n,)),
                pltpu.SemaphoreType.DMA((n,)),
            ],
            compiler_params=pltpu.CompilerParams(
                collective_id=0, has_side_effects=True, vmem_limit_bytes=63 * 1024 * 1024
            ),
        )(
            propagator.reshape(slots, width, cells),
            tile_blocks.T,
            histories.transpose(1, 0, 2).reshape(owned * tracers, sources),
        )
        return out.reshape(owned, tracers, months, cells)

    in_specs = (
        P(("groups", "tm"), None, None, "cells"),
        P(("groups", "tm"), None),
        P("tm", None, None),
    )
    out_specs = P(("groups", "tm"), None, None, "cells")
    return jax.shard_map(shards, mesh=mesh, in_specs=in_specs, out_specs=out_specs, check_vma=False)
```

```python
import functools

import jax
import jax.numpy as jnp
from jax import lax
from jax.experimental import pallas as pl
from jax.experimental.pallas import tpu as pltpu
from jax.sharding import PartitionSpec as P

MESH = pl.DeviceIdType.MESH
HALF = 64


def steps(low, high, body):
    if high - low <= 18:
        for index in reversed(range(low, high)):
            body(index)
    else:
        lax.fori_loop(low, high, lambda index, carry: (body(index), carry)[1], 0)


def iota(shape, dim):
    return lax.broadcasted_iota(jnp.int32, shape, dim)


def one_hot(condition):
    return jnp.where(condition, 1.0, 0.0).astype(jnp.bfloat16)


def dot(a, b):
    return jnp.dot(a, b, preferred_element_type=jnp.float32)


def encode(values):
    groups = values.reshape(-1, 8, 128)
    largest = jnp.max(jnp.abs(groups), axis=0)
    exponent = jnp.floor(jnp.log2(jnp.maximum(largest, 1e-37)))
    half = jnp.exp2(-0.5 * exponent)
    bits = exponent.astype(jnp.int32) + 128
    coded = []
    for i in range(groups.shape[0]):
        scaled = groups[i] * half * half * 8192.0
        code = jnp.clip(jnp.floor(scaled + 0.5), -16383.0, 16383.0).astype(jnp.int32) * 2
        if i < 8:
            code = code + ((bits >> i) & 1)
        coded.append(code)
    return jnp.concatenate(coded, axis=0).astype(jnp.int16)


def decode(code):
    groups = code.astype(jnp.int32).reshape(-1, 8, 128)
    low = groups & 1
    bits = low[0]
    for i in range(1, 8):
        bits = bits + (low[i] << i)
    half = jnp.exp2(0.5 * (bits - 128).astype(jnp.float32))
    values = (groups - low).astype(jnp.float32) * (1.0 / 16384.0) * half * half
    return values.reshape(2, -1, 128)


def partner(me, d, n):
    if n & (n - 1):
        return lax.rem(me + d, n)
    other, bit = 0, 1
    while bit < n:
        other = other + bit * ((me // bit + d // bit) % 2)
        bit *= 2
    return other


def kernel(
    n, months, prop_hbm, blocks_hbm, hist_hbm, out,
    prop, blocks, hist, message, held, expanded, outgoing, incoming, first, second,
    prop_sem, blocks_sem, hist_sem, hist_send, hist_recv, part_send, part_recv,
):
    me = lax.axis_index("tm")
    slots = blocks.shape[1]
    count = 2 * n
    rows = out.shape[1]
    tracers = rows // months
    width = prop.shape[1]
    months_held = hist.shape[1]

    barrier = pltpu.get_barrier_semaphore()

    def greet(d):
        pl.semaphore_signal(
            barrier, inc=1, device_id={"tm": partner(me, d, n)}, device_id_type=MESH
        )

    steps(1, n, greet)

    load_hist = pltpu.make_async_copy(hist_hbm, hist, hist_sem)
    load_hist.start()
    load_blocks = pltpu.make_async_copy(blocks_hbm, blocks, blocks_sem)
    load_blocks.start()
    load = pltpu.make_async_copy(prop_hbm, prop.at[:slots], prop_sem)
    load.start()

    pick = iota((16, 2 * tracers), 1)
    row = iota((16, 2 * tracers), 0)
    to_lane = iota((months_held, 128), 1) - iota((months_held, 128), 0)
    load_hist.wait()
    packed = jnp.zeros((16, 128), jnp.float32)
    for j in range(2):
        block = dot(one_hot(pick == 2 * row + j), hist[...]).astype(jnp.bfloat16)
        packed += dot(block, one_hot(to_lane == j * HALF))
    message[...] = packed.astype(jnp.bfloat16)
    held[me] = message[...]

    wide = 2 * rows
    tall_row = iota((wide, 32), 0)
    late = jnp.where(tall_row >= rows, 1, 0)
    wanted = (tall_row - late * rows) // months + 16 * late
    raise_rows = one_hot(iota((wide, 32), 1) == wanted)
    spread = one_hot(iota((128, width), 0) % HALF == iota((128, width), 1) // months)
    month = iota((rows, width), 0) % months == iota((rows, width), 1) % months
    prop[slots] = jnp.zeros((width, 128), jnp.bfloat16)

    pl.semaphore_wait(barrier, n - 1)

    def hist_copy(d):
        return pltpu.make_async_remote_copy(
            src_ref=message,
            dst_ref=held.at[me],
            send_sem=hist_send.at[d],
            recv_sem=hist_recv.at[d],
            device_id={"tm": partner(me, d, n)},
            device_id_type=MESH,
        )

    steps(1, n, lambda d: hist_copy(d).start())

    load_blocks.wait()

    p = blocks[0, 0]
    q = count - 1 - p

    def find(block):
        def look(slot, found):
            from_p, from_q = found
            hit = blocks[1, slot] == block
            is_p = blocks[0, slot] == p
            return (
                jnp.where(hit & is_p, slot, from_p),
                jnp.where(hit & jnp.logical_not(is_p), slot, from_q),
            )

        found = (jnp.int32(slots), jnp.int32(slots))
        if slots <= 18:
            for slot in range(slots):
                found = look(slot, found)
        else:
            found = lax.fori_loop(0, slots, look, found)
        first[block], second[block] = found

    steps(0, count, find)

    side = jnp.where(iota((wide, 128), 0) >= rows, q % 2, p % 2)
    keep = iota((wide, 128), 1) // HALF == side
    steps(1, n, lambda d: hist_copy(d).wait_recv())
    two = jnp.concatenate([held[p // 2], held[q // 2]], axis=0)
    tall = jnp.where(keep, dot(raise_rows, two), 0.0).astype(jnp.bfloat16)
    full = dot(tall, spread)
    for j in range(2):
        part = jnp.where(month, full[j * rows : (j + 1) * rows], 0.0)
        expanded[j] = part.astype(jnp.bfloat16)

    load.wait()

    def partial(block):
        return dot(expanded[0], prop[first[block]]) + dot(expanded[1], prop[second[block]])

    def part_copy(d):
        return pltpu.make_async_remote_copy(
            src_ref=outgoing.at[d],
            dst_ref=incoming.at[d],
            send_sem=part_send.at[d],
            recv_sem=part_recv.at[d],
            device_id={"tm": partner(me, d, n)},
            device_id_type=MESH,
        )

    def send(d):
        to = partner(me, d, n)
        both = jnp.concatenate([partial(2 * to), partial(2 * to + 1)], axis=0)
        outgoing[d] = encode(both)
        part_copy(d).start()

    steps(1, n, send)
    for j in range(2):
        out[j] = partial(2 * me + j)

    def receive(d):
        part_copy(d).wait_recv()
        out[...] += decode(incoming[d])

    steps(1, n, receive)

    def drain(d):
        hist_copy(d).wait_send()
        part_copy(d).wait_send()

    steps(1, n, drain)


def solution(mesh):
    n = mesh.shape["tm"]

    def shards(propagator, tile_blocks, histories):
        slots, sources, months, cells = propagator.shape
        owned, tracers, _ = histories.shape
        rows = tracers * months
        width = sources * months
        out = pl.pallas_call(
            functools.partial(kernel, n, months),
            out_shape=pltpu.VMEM((owned, rows, cells), jnp.float32),
            in_specs=[
                pl.BlockSpec(memory_space=pltpu.HBM),
                pl.BlockSpec(memory_space=pltpu.HBM),
                pl.BlockSpec(memory_space=pltpu.HBM),
            ],
            out_specs=pl.BlockSpec(memory_space=pltpu.VMEM),
            scratch_shapes=[
                pltpu.VMEM((slots + 1, width, cells), jnp.bfloat16),
                pltpu.SMEM((2, slots), jnp.int32),
                pltpu.VMEM((owned * tracers, sources), jnp.bfloat16),
                pltpu.VMEM((16, 128), jnp.bfloat16),
                pltpu.VMEM((n, 16, 128), jnp.bfloat16),
                pltpu.VMEM((2, rows, width), jnp.bfloat16),
                pltpu.VMEM((n, owned * rows, cells), jnp.int16),
                pltpu.VMEM((n, owned * rows, cells), jnp.int16),
                pltpu.SMEM((2 * n,), jnp.int32),
                pltpu.SMEM((2 * n,), jnp.int32),
                pltpu.SemaphoreType.DMA,
                pltpu.SemaphoreType.DMA,
                pltpu.SemaphoreType.DMA,
                pltpu.SemaphoreType.DMA((n,)),
                pltpu.SemaphoreType.DMA((n,)),
                pltpu.SemaphoreType.DMA((n,)),
                pltpu.SemaphoreType.DMA((n,)),
            ],
            compiler_params=pltpu.CompilerParams(
                collective_id=0, has_side_effects=True, vmem_limit_bytes=63 * 1024 * 1024
            ),
        )(
            propagator.reshape(slots, width, cells),
            tile_blocks.T,
            histories.transpose(1, 0, 2).reshape(owned * tracers, sources),
        )
        return out.reshape(owned, tracers, months, cells)

    in_specs = (
        P(("groups", "tm"), None, None, "cells"),
        P(("groups", "tm"), None),
        P("tm", None, None),
    )
    out_specs = P(("groups", "tm"), None, None, "cells")
    return jax.shard_map(shards, mesh=mesh, in_specs=in_specs, out_specs=out_specs, check_vma=False)
```

```python
import functools

import jax
import jax.numpy as jnp
from jax import lax
from jax.experimental import pallas as pl
from jax.experimental.pallas import tpu as pltpu
from jax.sharding import PartitionSpec as P

MESH = pl.DeviceIdType.MESH
HALF = 64


def steps(low, high, body):
    if high - low <= 18:
        for index in reversed(range(low, high)):
            body(index)
    else:
        lax.fori_loop(low, high, lambda index, carry: (body(index), carry)[1], 0)


def iota(shape, dim):
    return lax.broadcasted_iota(jnp.int32, shape, dim)


def one_hot(condition):
    return jnp.where(condition, 1.0, 0.0).astype(jnp.bfloat16)


def dot(a, b):
    return jnp.dot(a, b, preferred_element_type=jnp.float32)


def encode(values):
    groups = values.reshape(-1, 8, 128)
    largest = jnp.max(jnp.abs(groups), axis=0)
    exponent = jnp.floor(jnp.log2(jnp.maximum(largest, 1e-37)))
    half = jnp.exp2(-0.5 * exponent)
    bits = exponent.astype(jnp.int32) + 128
    coded = []
    for i in range(groups.shape[0]):
        scaled = groups[i] * half * half * 8192.0
        code = jnp.clip(jnp.floor(scaled + 0.5), -16383.0, 16383.0).astype(jnp.int32) * 2
        if i < 8:
            code = code + ((bits >> i) & 1)
        coded.append(code)
    return jnp.concatenate(coded, axis=0).astype(jnp.int16)


def decode(code):
    groups = code.astype(jnp.int32).reshape(-1, 8, 128)
    low = groups & 1
    bits = low[0]
    for i in range(1, 8):
        bits = bits + (low[i] << i)
    half = jnp.exp2(0.5 * (bits - 128).astype(jnp.float32))
    values = (groups - low).astype(jnp.float32) * (1.0 / 16384.0) * half * half
    return values.reshape(2, -1, 128)


def partner(me, d, n):
    if n & (n - 1):
        return lax.rem(me + d, n)
    other, bit = 0, 1
    while bit < n:
        other = other + bit * ((me // bit + d // bit) % 2)
        bit *= 2
    return other


def kernel(
    n, months, prop_hbm, blocks_hbm, hist_hbm, out,
    prop, blocks, hist, message, held, expanded, outgoing, incoming, first, second,
    prop_sem, blocks_sem, hist_sem, hist_send, hist_recv, part_send, part_recv,
):
    me = lax.axis_index("tm")
    slots = blocks.shape[1]
    count = 2 * n
    rows = out.shape[1]
    tracers = rows // months
    width = prop.shape[1]
    months_held = hist.shape[1]

    barrier = pltpu.get_barrier_semaphore()

    def greet(d):
        pl.semaphore_signal(
            barrier, inc=1, device_id={"tm": partner(me, d, n)}, device_id_type=MESH
        )

    steps(1, n, greet)

    load_hist = pltpu.make_async_copy(hist_hbm, hist, hist_sem)
    load_hist.start()
    load_blocks = pltpu.make_async_copy(blocks_hbm, blocks, blocks_sem)
    load_blocks.start()
    load = pltpu.make_async_copy(prop_hbm, prop.at[:slots], prop_sem)

    pick = iota((16, 2 * tracers), 1)
    row = iota((16, 2 * tracers), 0)
    to_lane = iota((months_held, 128), 1) - iota((months_held, 128), 0)
    load_hist.wait()
    packed = jnp.zeros((16, 128), jnp.float32)
    for j in range(2):
        block = dot(one_hot(pick == 2 * row + j), hist[...]).astype(jnp.bfloat16)
        packed += dot(block, one_hot(to_lane == j * HALF))
    message[...] = packed.astype(jnp.bfloat16)
    held[me] = message[...]

    wide = 2 * rows
    tall_row = iota((wide, 32), 0)
    late = jnp.where(tall_row >= rows, 1, 0)
    wanted = (tall_row - late * rows) // months + 16 * late
    raise_rows = one_hot(iota((wide, 32), 1) == wanted)
    spread = one_hot(iota((128, width), 0) % HALF == iota((128, width), 1) // months)
    month = iota((rows, width), 0) % months == iota((rows, width), 1) % months
    prop[slots] = jnp.zeros((width, 128), jnp.bfloat16)

    pl.semaphore_wait(barrier, n - 1)

    def hist_copy(d):
        return pltpu.make_async_remote_copy(
            src_ref=message,
            dst_ref=held.at[me],
            send_sem=hist_send.at[d],
            recv_sem=hist_recv.at[d],
            device_id={"tm": partner(me, d, n)},
            device_id_type=MESH,
        )

    steps(1, n, lambda d: hist_copy(d).start())
    load.start()

    load_blocks.wait()

    p = blocks[0, 0]
    q = count - 1 - p

    def find(block):
        def look(slot, found):
            from_p, from_q = found
            hit = blocks[1, slot] == block
            is_p = blocks[0, slot] == p
            return (
                jnp.where(hit & is_p, slot, from_p),
                jnp.where(hit & jnp.logical_not(is_p), slot, from_q),
            )

        found = (jnp.int32(slots), jnp.int32(slots))
        if slots <= 18:
            for slot in range(slots):
                found = look(slot, found)
        else:
            found = lax.fori_loop(0, slots, look, found)
        first[block], second[block] = found

    steps(0, count, find)

    side = jnp.where(iota((wide, 128), 0) >= rows, q % 2, p % 2)
    keep = iota((wide, 128), 1) // HALF == side
    steps(1, n, lambda d: hist_copy(d).wait_recv())
    two = jnp.concatenate([held[p // 2], held[q // 2]], axis=0)
    tall = jnp.where(keep, dot(raise_rows, two), 0.0).astype(jnp.bfloat16)
    full = dot(tall, spread)
    for j in range(2):
        part = jnp.where(month, full[j * rows : (j + 1) * rows], 0.0)
        expanded[j] = part.astype(jnp.bfloat16)

    load.wait()

    def partial(block):
        return dot(expanded[0], prop[first[block]]) + dot(expanded[1], prop[second[block]])

    def part_copy(d):
        return pltpu.make_async_remote_copy(
            src_ref=outgoing.at[d],
            dst_ref=incoming.at[d],
            send_sem=part_send.at[d],
            recv_sem=part_recv.at[d],
            device_id={"tm": partner(me, d, n)},
            device_id_type=MESH,
        )

    def send(d):
        to = partner(me, d, n)
        both = jnp.concatenate([partial(2 * to), partial(2 * to + 1)], axis=0)
        outgoing[d] = encode(both)
        part_copy(d).start()

    steps(1, n, send)
    for j in range(2):
        out[j] = partial(2 * me + j)

    def receive(d):
        part_copy(d).wait_recv()
        out[...] += decode(incoming[d])

    steps(1, n, lambda d: receive(n - d))

    def drain(d):
        hist_copy(d).wait_send()
        part_copy(d).wait_send()

    steps(1, n, drain)


def solution(mesh):
    n = mesh.shape["tm"]

    def shards(propagator, tile_blocks, histories):
        slots, sources, months, cells = propagator.shape
        owned, tracers, _ = histories.shape
        rows = tracers * months
        width = sources * months
        out = pl.pallas_call(
            functools.partial(kernel, n, months),
            out_shape=pltpu.VMEM((owned, rows, cells), jnp.float32),
            in_specs=[
                pl.BlockSpec(memory_space=pltpu.HBM),
                pl.BlockSpec(memory_space=pltpu.HBM),
                pl.BlockSpec(memory_space=pltpu.HBM),
            ],
            out_specs=pl.BlockSpec(memory_space=pltpu.VMEM),
            scratch_shapes=[
                pltpu.VMEM((slots + 1, width, cells), jnp.bfloat16),
                pltpu.SMEM((2, slots), jnp.int32),
                pltpu.VMEM((owned * tracers, sources), jnp.bfloat16),
                pltpu.VMEM((16, 128), jnp.bfloat16),
                pltpu.VMEM((n, 16, 128), jnp.bfloat16),
                pltpu.VMEM((2, rows, width), jnp.bfloat16),
                pltpu.VMEM((n, owned * rows, cells), jnp.int16),
                pltpu.VMEM((n, owned * rows, cells), jnp.int16),
                pltpu.SMEM((2 * n,), jnp.int32),
                pltpu.SMEM((2 * n,), jnp.int32),
                pltpu.SemaphoreType.DMA,
                pltpu.SemaphoreType.DMA,
                pltpu.SemaphoreType.DMA,
                pltpu.SemaphoreType.DMA((n,)),
                pltpu.SemaphoreType.DMA((n,)),
                pltpu.SemaphoreType.DMA((n,)),
                pltpu.SemaphoreType.DMA((n,)),
            ],
            compiler_params=pltpu.CompilerParams(
                collective_id=0, has_side_effects=True, vmem_limit_bytes=63 * 1024 * 1024
            ),
        )(
            propagator.reshape(slots, width, cells),
            tile_blocks.T,
            histories.transpose(1, 0, 2).reshape(owned * tracers, sources),
        )
        return out.reshape(owned, tracers, months, cells)

    in_specs = (
        P(("groups", "tm"), None, None, "cells"),
        P(("groups", "tm"), None),
        P("tm", None, None),
    )
    out_specs = P(("groups", "tm"), None, None, "cells")
    return jax.shard_map(shards, mesh=mesh, in_specs=in_specs, out_specs=out_specs, check_vma=False)
```

```python
import functools

import jax
import jax.numpy as jnp
from jax import lax
from jax.experimental import pallas as pl
from jax.experimental.pallas import tpu as pltpu
from jax.sharding import PartitionSpec as P

MESH = pl.DeviceIdType.MESH
HALF = 64


def steps(low, high, body):
    if high - low <= 18:
        for index in reversed(range(low, high)):
            body(index)
    else:
        lax.fori_loop(low, high, lambda index, carry: (body(index), carry)[1], 0)


def iota(shape, dim):
    return lax.broadcasted_iota(jnp.int32, shape, dim)


def one_hot(condition):
    return jnp.where(condition, 1.0, 0.0).astype(jnp.bfloat16)


def dot(a, b):
    return jnp.dot(a, b, preferred_element_type=jnp.float32)


def encode(values):
    groups = values.reshape(-1, 8, 128)
    largest = jnp.max(jnp.abs(groups), axis=0)
    exponent = jnp.floor(jnp.log2(jnp.maximum(largest, 1e-37)))
    half = jnp.exp2(-0.5 * exponent)
    bits = exponent.astype(jnp.int32) + 128
    coded = []
    for i in range(groups.shape[0]):
        scaled = groups[i] * half * half * 8192.0
        code = jnp.clip(jnp.floor(scaled + 0.5), -16383.0, 16383.0).astype(jnp.int32) * 2
        if i < 8:
            code = code + ((bits >> i) & 1)
        coded.append(code)
    return jnp.concatenate(coded, axis=0).astype(jnp.int16)


def decode(code):
    groups = code.astype(jnp.int32).reshape(-1, 8, 128)
    low = groups & 1
    bits = low[0]
    for i in range(1, 8):
        bits = bits + (low[i] << i)
    half = jnp.exp2(0.5 * (bits - 128).astype(jnp.float32))
    values = (groups - low).astype(jnp.float32) * (1.0 / 16384.0) * half * half
    return values.reshape(2, -1, 128)


def partner(me, d, n):
    if n & (n - 1):
        return lax.rem(me + d, n)
    other, bit = 0, 1
    while bit < n:
        other = other + bit * ((me // bit + d // bit) % 2)
        bit *= 2
    return other


def kernel(
    n, months, prop_hbm, blocks_hbm, hist_hbm, out,
    prop, blocks, hist, message, held, outgoing, incoming, first, second,
    prop_sem, blocks_sem, hist_sem, hist_send, hist_recv, part_send, part_recv,
):
    me = lax.axis_index("tm")
    slots = blocks.shape[1]
    count = 2 * n
    rows = out.shape[1]
    tracers = rows // months
    width = prop.shape[1]
    months_held = hist.shape[1]

    barrier = pltpu.get_barrier_semaphore()

    def greet(d):
        pl.semaphore_signal(
            barrier, inc=1, device_id={"tm": partner(me, d, n)}, device_id_type=MESH
        )

    steps(1, n, greet)

    load_hist = pltpu.make_async_copy(hist_hbm, hist, hist_sem)
    load_hist.start()
    load_blocks = pltpu.make_async_copy(blocks_hbm, blocks, blocks_sem)
    load_blocks.start()
    load = pltpu.make_async_copy(prop_hbm, prop.at[:slots], prop_sem)
    load.start()

    pick = iota((16, 2 * tracers), 1)
    row = iota((16, 2 * tracers), 0)
    to_lane = iota((months_held, 128), 1) - iota((months_held, 128), 0)
    load_hist.wait()
    packed = jnp.zeros((16, 128), jnp.float32)
    for j in range(2):
        block = dot(one_hot(pick == 2 * row + j), hist[...]).astype(jnp.bfloat16)
        packed += dot(block, one_hot(to_lane == j * HALF))
    message[...] = packed.astype(jnp.bfloat16)
    held[me] = message[...]

    wide = 2 * rows
    tall_row = iota((wide, 32), 0)
    late = jnp.where(tall_row >= rows, 1, 0)
    wanted = (tall_row - late * rows) // months + 16 * late
    raise_rows = one_hot(iota((wide, 32), 1) == wanted)
    spread = one_hot(iota((128, width), 0) % HALF == iota((128, width), 1) // months)
    month = iota((rows, width), 0) % months == iota((rows, width), 1) % months
    prop[slots] = jnp.zeros((width, 128), jnp.bfloat16)

    pl.semaphore_wait(barrier, n - 1)

    def hist_copy(d):
        return pltpu.make_async_remote_copy(
            src_ref=message,
            dst_ref=held.at[me],
            send_sem=hist_send.at[d],
            recv_sem=hist_recv.at[d],
            device_id={"tm": partner(me, d, n)},
            device_id_type=MESH,
        )

    steps(1, n, lambda d: hist_copy(d).start())

    load_blocks.wait()

    p = blocks[0, 0]
    q = count - 1 - p

    def find(block):
        def look(slot, found):
            from_p, from_q = found
            hit = blocks[1, slot] == block
            is_p = blocks[0, slot] == p
            return (
                jnp.where(hit & is_p, slot, from_p),
                jnp.where(hit & jnp.logical_not(is_p), slot, from_q),
            )

        found = (jnp.int32(slots), jnp.int32(slots))
        if slots <= 18:
            for slot in range(slots):
                found = look(slot, found)
        else:
            found = lax.fori_loop(0, slots, look, found)
        first[block], second[block] = found

    steps(0, count, find)

    side = jnp.where(iota((wide, 128), 0) >= rows, q % 2, p % 2)
    keep = iota((wide, 128), 1) // HALF == side
    steps(1, n, lambda d: hist_copy(d).wait_recv())
    two = jnp.concatenate([held[p // 2], held[q // 2]], axis=0)
    tall = jnp.where(keep, dot(raise_rows, two), 0.0).astype(jnp.bfloat16)
    full = dot(tall, spread)
    sides = []
    for j in range(2):
        part = jnp.where(month, full[j * rows : (j + 1) * rows], 0.0)
        sides.append(part.astype(jnp.bfloat16))

    load.wait()

    def partial(block):
        return dot(sides[0], prop[first[block]]) + dot(sides[1], prop[second[block]])

    def part_copy(d):
        return pltpu.make_async_remote_copy(
            src_ref=outgoing.at[d],
            dst_ref=incoming.at[d],
            send_sem=part_send.at[d],
            recv_sem=part_recv.at[d],
            device_id={"tm": partner(me, d, n)},
            device_id_type=MESH,
        )

    def send(d):
        to = partner(me, d, n)
        both = jnp.concatenate([partial(2 * to), partial(2 * to + 1)], axis=0)
        outgoing[d] = encode(both)
        part_copy(d).start()

    steps(1, n, send)
    for j in range(2):
        out[j] = partial(2 * me + j)

    def receive(d):
        part_copy(d).wait_recv()
        out[...] += decode(incoming[d])

    steps(1, n, receive)

    def drain(d):
        hist_copy(d).wait_send()
        part_copy(d).wait_send()

    steps(1, n, drain)


def solution(mesh):
    n = mesh.shape["tm"]

    def shards(propagator, tile_blocks, histories):
        slots, sources, months, cells = propagator.shape
        owned, tracers, _ = histories.shape
        rows = tracers * months
        width = sources * months
        out = pl.pallas_call(
            functools.partial(kernel, n, months),
            out_shape=pltpu.VMEM((owned, rows, cells), jnp.float32),
            in_specs=[
                pl.BlockSpec(memory_space=pltpu.HBM),
                pl.BlockSpec(memory_space=pltpu.HBM),
                pl.BlockSpec(memory_space=pltpu.HBM),
            ],
            out_specs=pl.BlockSpec(memory_space=pltpu.VMEM),
            scratch_shapes=[
                pltpu.VMEM((slots + 1, width, cells), jnp.bfloat16),
                pltpu.SMEM((2, slots), jnp.int32),
                pltpu.VMEM((owned * tracers, sources), jnp.bfloat16),
                pltpu.VMEM((16, 128), jnp.bfloat16),
                pltpu.VMEM((n, 16, 128), jnp.bfloat16),
                pltpu.VMEM((n, owned * rows, cells), jnp.int16),
                pltpu.VMEM((n, owned * rows, cells), jnp.int16),
                pltpu.SMEM((2 * n,), jnp.int32),
                pltpu.SMEM((2 * n,), jnp.int32),
                pltpu.SemaphoreType.DMA,
                pltpu.SemaphoreType.DMA,
                pltpu.SemaphoreType.DMA,
                pltpu.SemaphoreType.DMA((n,)),
                pltpu.SemaphoreType.DMA((n,)),
                pltpu.SemaphoreType.DMA((n,)),
                pltpu.SemaphoreType.DMA((n,)),
            ],
            compiler_params=pltpu.CompilerParams(
                collective_id=0, has_side_effects=True, vmem_limit_bytes=63 * 1024 * 1024
            ),
        )(
            propagator.reshape(slots, width, cells),
            tile_blocks.T,
            histories.transpose(1, 0, 2).reshape(owned * tracers, sources),
        )
        return out.reshape(owned, tracers, months, cells)

    in_specs = (
        P(("groups", "tm"), None, None, "cells"),
        P(("groups", "tm"), None),
        P("tm", None, None),
    )
    out_specs = P(("groups", "tm"), None, None, "cells")
    return jax.shard_map(shards, mesh=mesh, in_specs=in_specs, out_specs=out_specs, check_vma=False)
```
